128 devices in a mesh: lon: 64 (over y, z_lo, x, core), lat: 2 (over z_hi).
Axes of the slice: x: 4, y: 4, z: 4 (z_hi: 2, z_lo: 2; z = z_hi * 2 + z_lo), core: 2. Of those that a mesh axis runs over, the one named last changes fastest.
Arguments:
- surface: float32 [64, 655360], P('lon'), may hold values from -6 to 6
- fidelity: float32 [64, 655360], P('lon'), may hold values from 0.5 to 4
- smoothing: float32 [64, 655360], P('lat', 'lon'), may hold values from 0.1 to 1
Outputs:
- heights: float32 [64, 655360], P('lat', 'lon')
- dual_x: float32 [64, 655360], P('lat', 'lon')
- dual_y: float32 [64, 655360], P('lat', 'lon')
- gap: float32 [3], replicated
The draws below stay inside these ranges and needn't reach their ends.
All inputs are finite; a program needn't handle non-finite values.
Results may differ from the reference program's by a relative error of at most 0.0001.
Values sent between devices are 32-bit elements; how exact they have to be, the bound alone decides.
A program may use at most 128 MiB of HBM per device.

```python
import math
import jax
import jax.numpy as jnp

ITERS = 3
NR = 64
NC = 655360


def level_of(own_key, extent, shards, low, high):
    loudness = 1.0
    for axis_at, parts in shards:
        draws = jax.random.uniform(jax.random.fold_in(jax.random.fold_in(own_key, 6), axis_at), (parts,), jnp.float32, low / len(shards), high / len(shards))
        loudness = loudness * jnp.repeat(jnp.exp(draws), extent[axis_at] // parts).reshape((-1,) + (1,) * (len(extent) - 1 - axis_at))
    return loudness


def bell_draw(rng, shape, spread, reach, shards=(), kind=jnp.bfloat16):
    values = jax.random.normal(rng, shape, jnp.float32) * spread
    if len(shards) > 0:
        values = level_of(rng, shape, shards, -0.22, 0.18) * values
    return jnp.clip(values, min=-reach, max=reach).astype(kind)


def setup_inputs(seed: int = 0) -> dict:
    key_of = jax.random.split(jax.random.key(seed), 4)
    return {
        "surface": bell_draw(key_of[0], (NR, NC), 1.0, 6.0, ((0, 64),), jnp.float32),
        "fidelity": jnp.clip(jnp.exp(math.log(4.0) - 2.0794415 * jax.random.uniform(key_of[1], (NR, NC), jnp.float32) ** level_of(key_of[1], (NR, NC), ((0, 64),), -0.2, 0.2)), 0.5, 4.0),
        "smoothing": jnp.clip(jnp.exp(math.log(1.0) - 2.3025851 * jax.random.uniform(key_of[2], (NR, NC), jnp.float32) ** level_of(key_of[2], (NR, NC), ((0, 2), (1, 64)), -0.2, 0.2)), 0.1, 1.0),
    }


primal_step = 0.35
dual_step = 0.35

def forward_diff(field):
    grad_x = jnp.roll(field, -1, axis=1) - field
    grad_y = jnp.concatenate([field[1:] - field[:-1], jnp.zeros((1, field.shape[1]), field.dtype)], axis=0)
    return (grad_x, grad_y)

def divergence(dual_x, dual_y):
    part_x = dual_x - jnp.roll(dual_x, 1, axis=1)
    upper = jnp.concatenate([jnp.zeros((1, dual_y.shape[1]), dual_y.dtype), dual_y[:-1]], axis=0)
    return part_x + dual_y - upper

def reference(surface, fidelity, smoothing):
    heights = surface
    lead = surface
    dual_x = jnp.zeros_like(surface)
    dual_y = jnp.zeros_like(surface)
    cells = NR * NC
    gaps = []
    for step in range(ITERS):
        grad_x, grad_y = forward_diff(lead)
        cand_x = dual_x + dual_step * grad_x
        cand_y = dual_y + dual_step * grad_y
        shrink = jnp.maximum(1.0, jnp.sqrt(cand_x * cand_x + cand_y * cand_y) / smoothing)
        dual_x = cand_x / shrink
        dual_y = cand_y / shrink
        diverge = divergence(dual_x, dual_y)
        slope_x, slope_y = forward_diff(heights)
        misfit = heights - surface
        terms = 0.5 * fidelity * misfit * misfit + smoothing * jnp.sqrt(slope_x * slope_x + slope_y * slope_y) + surface * diverge + 0.5 * diverge * diverge / fidelity
        gaps.append(jnp.sum(terms) / cells)
        updated = (heights + primal_step * diverge + primal_step * fidelity * surface) / (1.0 + primal_step * fidelity)
        lead = 2.0 * updated - heights
        heights = updated
    return (heights, dual_x, dual_y, jnp.stack(gaps))
```

```python
import functools

import jax
import jax.numpy as jnp
from jax import lax
from jax.experimental import pallas as pl
from jax.experimental.pallas import tpu as pltpu
from jax.sharding import PartitionSpec as P

MESH = pl.DeviceIdType.MESH
STEP = 0.35
ITERS = 3
LANES = 128
ROWS = 32
CHUNKS = 80
LINE = 5120
WIN = 35
HALO = 15
PITCH = 112
CUTS = (0, 42, 66, 82)
PARTS = len(CUTS) - 1
FIRST, LAST = 1, 12


def kernel(
    surf_hbm, fid_hbm, smooth_hbm,
    out_h, out_x, out_y, gap_out,
    surf, fid, wgt, tile_in, height, dual_x, dual_y, slope_x, slope_y,
    acc, slots_a, slots_b,
    send_sem, recv_sem, relay_send, relay_recv, wrow_sem, wcol_sem, tile_sem, gap_send, gap_recv,
):
    lon = lax.axis_index("lon")
    lat = lax.axis_index("lat")
    core, x, zlo, y = lon % 2, (lon // 2) % 4, (lon // 8) % 2, lon // 16
    half = y // 2
    z_to = (zlo + lat + half) % 2
    own = lat == half
    slot = lon - 29 * half
    first = 3 * lat

    def lon_of(y_, zlo_, x_, core_):
        return ((y_ * 2 + zlo_) * 4 + x_) * 2 + core_

    tile_copy = pltpu.make_async_copy(smooth_hbm, tile_in, tile_sem)
    tile_copy.start()

    barrier = pltpu.get_barrier_semaphore()

    def greet(lon_, lat_):
        pl.semaphore_signal(barrier, inc=1, device_id=(lon_, lat_), device_id_type=MESH)

    def greet_source(k, carry):
        zs = (zlo + k) % 2
        zh = jnp.where(zs == zlo, lat, 1 - lat)
        src = lon_of(2 * lat + (k // 2) % 2, zs, (x + k // 8) % 4, (core + k // 4) % 2)

        @pl.when((src != lon) | (zh != lat))
        def _():
            greet(src, zh)

        return carry

    lax.fori_loop(0, 32, greet_source, 0)
    east, west = (lon + 1) % 64, (lon + 63) % 64
    greet(lon, 1 - lat)
    greet(east, lat)
    greet(west, lat)

    def peer_a(k):
        return lon_of(y, zlo, (x + k // 2) % 4, (core + k) % 2), lat

    def peer_b(k):
        return lon_of((y + k // 4) % 4, (zlo + k // 2) % 2, x, core), (lat + k) % 2

    def greet_a(k, carry):
        greet(*peer_a(k))
        return carry

    def greet_b(k, carry):
        greet(*peer_b(k))
        return carry

    lax.fori_loop(1, 8, greet_a, 0)
    lax.fori_loop(1, 16, greet_b, 0)

    tile_copy.wait()

    def lay(k, carry):
        blk, g = k // 10, k % 10
        for r8 in range(8):
            wgt[first + blk * 8 + r8, pl.ds(16 + 8 * g, 8), :] = tile_in[
                pl.ds(blk * 640 + g * 64 + r8, 8, stride=8), :
            ]
        return carry

    lax.fori_loop(0, 40, lay, 0)

    n_self = own.astype(jnp.int32)
    pl.semaphore_wait(barrier, 32 - n_self + 3 + 7 + 15)

    give = 29 - 26 * lat
    put = 32 * lat

    def row_copy(ref, lo, n, s_sem, r_sem):
        return pltpu.make_async_remote_copy(
            ref.at[pl.ds(give, 3), pl.ds(lo, n)],
            ref.at[pl.ds(put, 3), pl.ds(lo, n)],
            s_sem, r_sem, device_id=(lon, 1 - lat), device_id_type=MESH,
        )

    wrow = row_copy(wgt, HALO + 1, CHUNKS, wrow_sem.at[0], wrow_sem.at[1])
    wrow.start()

    def send_part(part):
        lo, hi = CUTS[part], CUTS[part + 1]

        def send(k, carry):
            dx = (k + 1) % 4
            dy = ((k % 16) // 4 + 4 - dx) % 4
            dst = lon_of((y + dy) % 4, z_to, (x + dx) % 4, (core + k // 16) % 2)
            here = (k == 3) & own

            def copy(i, a, b, at):
                src_ref = (surf_hbm, fid_hbm)[i].at[pl.ds(at, b - a)]
                dst_ref = (surf, fid)[i].at[slot, pl.ds(HALO + a, b - a)]

                @pl.when(here)
                def _():
                    pltpu.make_async_copy(src_ref, dst_ref, recv_sem.at[i, part]).start()

                @pl.when(jnp.logical_not(here))
                def _():
                    pltpu.make_async_remote_copy(
                        src_ref, dst_ref, send_sem.at[i], recv_sem.at[i, part],
                        device_id=(dst, half), device_id_type=MESH,
                    ).start()

            for i in range(2):
                start = dst * CHUNKS - 1
                if lo == 0:
                    @pl.when(dst == 0)
                    def _():
                        copy(i, 0, 1, LINE - 1)
                        copy(i, 1, hi, 0)

                    @pl.when(dst != 0)
                    def _():
                        copy(i, 0, hi, start)
                elif hi == CHUNKS + 2:
                    @pl.when(dst == 63)
                    def _():
                        copy(i, lo, hi - 1, LINE - CHUNKS - 1 + lo)
                        copy(i, hi - 1, hi, 0)

                    @pl.when(dst != 63)
                    def _():
                        copy(i, lo, hi, start + lo)
                else:
                    copy(i, lo, hi, start + lo)
            return carry

        lax.fori_loop(0, 32, send, 0)

    send_part(0)

    wrow.wait()
    wcols = [
        pltpu.make_async_remote_copy(
            wgt.at[pl.ds(0, WIN), pl.ds(at, 1)],
            wgt.at[pl.ds(0, WIN), pl.ds(to, 1)],
            wcol_sem.at[0, i], wcol_sem.at[1, i], device_id=(dev, lat), device_id_type=MESH,
        )
        for i, (at, to, dev) in enumerate(((HALO + CHUNKS, HALO, east), (HALO + 1, HALO + 1 + CHUNKS, west)))
    ]
    for c in wcols:
        c.start()
    for part in range(1, PARTS):
        send_part(part)

    lane = lax.broadcasted_iota(jnp.int32, (8, LANES), 1)
    is_first, is_last = lane == 0, lane == LANES - 1

    def at(ref, w, q):
        return ref[w, pl.ds(q, 8), :]

    def to_east(ref, w, q, mid):
        nxt = at(ref, w, q + 1)
        return pltpu.roll(jnp.where(is_first, nxt, mid), LANES - 1, 1)

    def to_west(ref, w, q, mid):
        prv = at(ref, w, q - 1)
        return pltpu.roll(jnp.where(is_last, prv, mid), 1, 1)

    def dual_row(step, w, q, mid, below):
        weight = at(wgt, w, q)
        ux = to_east(surf if step == 0 else height, w, q, mid) - mid
        uy = jnp.zeros_like(mid) if below is None else below - mid
        if step == 0:
            qx, qy = STEP * ux, STEP * uy
        else:
            qx = at(dual_x, w, q) + STEP * (2.0 * ux - at(slope_x, w, q))
            qy = at(dual_y, w, q) + STEP * (2.0 * uy - at(slope_y, w, q))
        if step < ITERS - 1:
            slope_x[w, pl.ds(q, 8), :] = ux
            slope_y[w, pl.ds(q, 8), :] = uy
        shrink = jnp.minimum(1.0, weight * lax.rsqrt(qx * qx + qy * qy))
        px, py = qx * shrink, qy * shrink
        dual_x[w, pl.ds(q, 8), :] = px
        dual_y[w, pl.ds(q, 8), :] = py
        return px, py, weight * jnp.sqrt(ux * ux + uy * uy)

    def primal_row(step, w, q, height_ref, py_north):
        px, py = at(dual_x, w, q), at(dual_y, w, q)
        d = px - to_west(dual_x, w, q, px) + py
        if py_north is not None:
            d = d - py_north
        h, s, f = at(height_ref, w, q), at(surf, w, q), at(fid, w, q)
        scaled = STEP * f
        damp = 1.0 + scaled
        both = 1.0 / (f * damp)
        term = d * (s + (0.5 * d) * (both * damp))
        if step > 0:
            miss = h - s
            term = term + (0.5 * f) * (miss * miss)
        new = (h + STEP * d + scaled * s) * (both * f)
        return py, new, term

    def masked(terms):
        low = jnp.where(lat == 0, terms[0] + terms[1] + terms[2], 0.0)
        top = jnp.where(lat == 1, terms[32] + terms[33] + terms[34], 0.0)
        return low + functools.reduce(jnp.add, terms[3:32]) + top

    def early(step, g0, g1):
        height_ref = surf if step == 0 else height

        def group(g, carry):
            q = pl.multiple_of(8 * g, 8)
            mid = at(height_ref, 0, q)
            terms = []
            for w in range(WIN):
                below = at(height_ref, w + 1, q) if w < WIN - 1 else None
                terms.append(dual_row(step, w, q, mid, below)[2])
                mid = below
            total = masked(terms)
            north = None
            terms = []
            for w in range(WIN):
                north, new, term = primal_row(step, w, q, height_ref, north)
                terms.append(term)
                height[w, pl.ds(q, 8), :] = new
            height[WIN, pl.ds(q, 8), :] = new
            in_tile = (g > FIRST) & (g < LAST)
            acc[step] += jnp.where(in_tile, total + masked(terms), 0.0)
            return carry

        if g1 > g0:
            lax.fori_loop(g0, g1, group, 0)

    def last_duals(q, place):
        mid = at(height, first, q)
        total = None
        for r in range(ROWS):
            w = first + r
            below = at(height, w + 1, q)
            px, py, term = dual_row(ITERS - 1, w, q, mid, below)
            if place is not None:
                out_x[place(r), :] = px
                out_y[place(r), :] = py
            total = term if total is None else total + term
            mid = below
        return total

    def last(g0, g1):
        def group(g, carry):
            q = pl.multiple_of(8 * g, 8)

            def place(r):
                return pl.ds(r // 8 * 640 + (g - FIRST - 1) * 64 + r % 8, 8, stride=8)

            w = jnp.where(lat == 0, WIN - 1, first - 1)
            north = dual_row(ITERS - 1, w, q, at(height, w, q), at(height, w + 1, q))[1]
            north = jnp.where(lat == 0, 0.0, north)
            total = last_duals(q, place)
            for r in range(ROWS):
                north, new, term = primal_row(ITERS - 1, first + r, q, height, north)
                out_h[place(r), :] = new
                total = total + term
            acc[ITERS - 1] += total
            return carry

        if g1 > g0:
            lax.fori_loop(g0, g1, group, 0)

    for step in range(ITERS):
        acc[step] = jnp.zeros((8, LANES), jnp.float32)

    done = FIRST
    for part in range(PARTS):
        lo, n = HALO + CUTS[part], CUTS[part + 1] - CUTS[part]
        for i, ref in enumerate((surf, fid)):
            got = ref.at[pl.ds(0, ROWS), pl.ds(lo, n)]
            pltpu.make_async_copy(got, got, recv_sem.at[i, part]).wait()
        relays = [
            row_copy(ref, lo, n, relay_send.at[i, part], relay_recv.at[i, part])
            for i, ref in enumerate((surf, fid))
        ]
        for c in relays:
            c.start()
        if part == 0:
            for c in wcols:
                c.wait()
        for c in relays:
            c.wait()

        final = part == PARTS - 1
        stop = LAST + 1 if final else (HALO + CUTS[part + 1] - 9) // 8 + 1
        early(0, done, stop)
        early(1, max(done - 1, FIRST), stop if final else stop - 1)
        if part == 0:
            last_duals(8 * FIRST, None)
        last(max(done - 2, FIRST + 1), stop - 1 if final else stop - 2)
        done = stop

    def total_of(ref, n):
        total = ref[0]
        for k in range(1, n):
            total = total + ref[k]
        return total

    rows = [jnp.sum(acc[step], axis=0, keepdims=True) for step in range(ITERS)]
    slots_a[0] = jnp.concatenate(rows + [jnp.zeros((5, LANES), jnp.float32)], axis=0)

    def spread(slots, n, peer, which):
        def go(k, carry):
            pltpu.make_async_remote_copy(
                slots.at[0], slots.at[k], gap_send.at[which], gap_recv.at[which],
                device_id=peer(k), device_id_type=MESH,
            ).start()
            return carry

        lax.fori_loop(1, n, go, 0)
        rest = slots.at[pl.ds(1, n - 1)]
        pltpu.make_async_copy(rest, rest, gap_recv.at[which]).wait()
        pltpu.make_async_copy(rest, rest, gap_send.at[which]).wait()

    spread(slots_a, 8, peer_a, 0)
    slots_b[0] = total_of(slots_a, 8)
    spread(slots_b, 16, peer_b, 1)
    gap_out[...] = jnp.sum(total_of(slots_b, 16), axis=1, keepdims=True) * (
        1.0 / (2 * ROWS * LINE * LANES)
    ) + jnp.zeros((8, LANES), jnp.float32)

    for i, ref in enumerate((surf, fid)):
        for n, cond in ((31, own), (32, jnp.logical_not(own))):
            @pl.when(cond)
            def _():
                sent = ref.at[pl.ds(0, n), pl.ds(0, CHUNKS + 2)]
                pltpu.make_async_copy(sent, sent, send_sem.at[i]).wait()


def on_device(surface, fidelity, smoothing):
    tile = smoothing.reshape(4, 8, CHUNKS, LANES).transpose(0, 2, 1, 3).reshape(-1, LANES)
    window = pltpu.VMEM((WIN + 1, PITCH, LANES), jnp.float32)
    flat = jax.ShapeDtypeStruct((ROWS * CHUNKS, LANES), jnp.float32)
    *outs, gap = pl.pallas_call(
        kernel,
        out_shape=[flat] * 3 + [jax.ShapeDtypeStruct((8, LANES), jnp.float32)],
        in_specs=[pl.BlockSpec(memory_space=pltpu.HBM)] * 3,
        out_specs=[pl.BlockSpec(memory_space=pltpu.VMEM)] * 4,
        scratch_shapes=[window] * 3
        + [pltpu.VMEM((ROWS * CHUNKS, LANES), jnp.float32)]
        + [window] * 5
        + [
            pltpu.VMEM((ITERS, 8, LANES), jnp.float32),
            pltpu.VMEM((8, 8, LANES), jnp.float32),
            pltpu.VMEM((16, 8, LANES), jnp.float32),
            pltpu.SemaphoreType.DMA((2,)),
            pltpu.SemaphoreType.DMA((2, PARTS)),
            pltpu.SemaphoreType.DMA((2, PARTS)),
            pltpu.SemaphoreType.DMA((2, PARTS)),
            pltpu.SemaphoreType.DMA((2,)),
            pltpu.SemaphoreType.DMA((2, 2)),
            pltpu.SemaphoreType.DMA,
            pltpu.SemaphoreType.DMA((2,)),
            pltpu.SemaphoreType.DMA((2,)),
        ],
        compiler_params=pltpu.CompilerParams(
            collective_id=0, has_side_effects=True, vmem_limit_bytes=48 * 2**20
        ),
    )(surface.reshape(LINE, LANES), fidelity.reshape(LINE, LANES), tile)
    tiles = [
        o.reshape(4, CHUNKS, 8, LANES).transpose(0, 2, 1, 3).reshape(ROWS, CHUNKS * LANES)
        for o in outs
    ]
    return (*tiles, gap[:ITERS, 0])


def solution(mesh):
    in_specs = (P("lon", None), P("lon", None), P("lat", "lon"))
    out_specs = (P("lat", "lon"), P("lat", "lon"), P("lat", "lon"), P())
    return jax.shard_map(
        on_device, mesh=mesh, in_specs=in_specs, out_specs=out_specs, check_vma=False
    )
```

```python
import functools

import jax
import jax.numpy as jnp
from jax import lax
from jax.experimental import pallas as pl
from jax.experimental.pallas import tpu as pltpu
from jax.sharding import PartitionSpec as P

MESH = pl.DeviceIdType.MESH
STEP = 0.35
ITERS = 3
LANES = 128
ROWS = 32
CHUNKS = 80
LINE = 5120
WIN = 35
HALO = 15
PITCH = 112
CUTS = (0, 42, 66, 82)
PARTS = len(CUTS) - 1
FIRST, LAST = 1, 12


def kernel(
    surf_hbm, fid_hbm, smooth_hbm,
    out_h, out_x, out_y, gap_out,
    surf, fid, wgt, tile_in, height, dual_x, dual_y, slope_x, slope_y,
    acc, slots_a, slots_b,
    send_sem, recv_sem, relay_send, relay_recv, wrow_sem, wcol_sem, tile_sem, gap_send, gap_recv,
):
    lon = lax.axis_index("lon")
    lat = lax.axis_index("lat")
    core, x, zlo, y = lon % 2, (lon // 2) % 4, (lon // 8) % 2, lon // 16
    half = y // 2
    z_to = (zlo + lat + half) % 2
    own = lat == half
    slot = lon - 29 * half
    first = 3 * lat

    def lon_of(y_, zlo_, x_, core_):
        return ((y_ * 2 + zlo_) * 4 + x_) * 2 + core_

    tile_copy = pltpu.make_async_copy(smooth_hbm, tile_in, tile_sem)
    tile_copy.start()

    barrier = pltpu.get_barrier_semaphore()

    def greet(lon_, lat_):
        pl.semaphore_signal(barrier, inc=1, device_id=(lon_, lat_), device_id_type=MESH)

    def greet_source(k, carry):
        zs = (zlo + k) % 2
        zh = jnp.where(zs == zlo, lat, 1 - lat)
        src = lon_of(2 * lat + (k // 2) % 2, zs, (x + k // 8) % 4, (core + k // 4) % 2)

        @pl.when((src != lon) | (zh != lat))
        def _():
            greet(src, zh)

        return carry

    lax.fori_loop(0, 32, greet_source, 0)
    east, west = (lon + 1) % 64, (lon + 63) % 64
    greet(lon, 1 - lat)
    greet(east, lat)
    greet(west, lat)

    def peer_a(k):
        return lon_of(y, zlo, (x + k // 2) % 4, (core + k) % 2), lat

    def peer_b(k):
        return lon_of((y + k // 4) % 4, (zlo + k // 2) % 2, x, core), (lat + k) % 2

    def greet_a(k, carry):
        greet(*peer_a(k))
        return carry

    def greet_b(k, carry):
        greet(*peer_b(k))
        return carry

    lax.fori_loop(1, 8, greet_a, 0)
    lax.fori_loop(1, 16, greet_b, 0)

    tile_copy.wait()

    def lay(k, carry):
        blk, g = k // 10, k % 10
        for r8 in range(8):
            wgt[first + blk * 8 + r8, pl.ds(16 + 8 * g, 8), :] = tile_in[
                pl.ds(blk * 640 + g * 64 + r8, 8, stride=8), :
            ]
        return carry

    lax.fori_loop(0, 40, lay, 0)

    n_self = own.astype(jnp.int32)
    pl.semaphore_wait(barrier, 32 - n_self + 3 + 7 + 15)

    def row_copy(ref, depth, lo, n, s_sem, r_sem):
        give = (32 - depth) * (1 - lat) + 3 * lat
        put = (3 - depth) * (1 - lat) + 32 * lat
        return pltpu.make_async_remote_copy(
            ref.at[pl.ds(give, depth), pl.ds(lo, n)],
            ref.at[pl.ds(put, depth), pl.ds(lo, n)],
            s_sem, r_sem, device_id=(lon, 1 - lat), device_id_type=MESH,
        )

    wrow = row_copy(wgt, 3, HALO + 1, CHUNKS, wrow_sem.at[0], wrow_sem.at[1])
    wrow.start()

    def send_part(part):
        lo, hi = CUTS[part], CUTS[part + 1]

        def send(k, carry):
            dx = (k + 1) % 4
            dy = ((k % 16) // 4 + 4 - dx) % 4
            dst = lon_of((y + dy) % 4, z_to, (x + dx) % 4, (core + k // 16) % 2)
            here = (k == 3) & own

            def copy(i, a, b, at):
                src_ref = (surf_hbm, fid_hbm)[i].at[pl.ds(at, b - a)]
                dst_ref = (surf, fid)[i].at[slot, pl.ds(HALO + a, b - a)]

                @pl.when(here)
                def _():
                    pltpu.make_async_copy(src_ref, dst_ref, recv_sem.at[i, part]).start()

                @pl.when(jnp.logical_not(here))
                def _():
                    pltpu.make_async_remote_copy(
                        src_ref, dst_ref, send_sem.at[i], recv_sem.at[i, part],
                        device_id=(dst, half), device_id_type=MESH,
                    ).start()

            for i in range(2):
                start = dst * CHUNKS - 1
                if lo == 0:
                    @pl.when(dst == 0)
                    def _():
                        copy(i, 0, 1, LINE - 1)
                        copy(i, 1, hi, 0)

                    @pl.when(dst != 0)
                    def _():
                        copy(i, 0, hi, start)
                elif hi == CHUNKS + 2:
                    @pl.when(dst == 63)
                    def _():
                        copy(i, lo, hi - 1, LINE - CHUNKS - 1 + lo)
                        copy(i, hi - 1, hi, 0)

                    @pl.when(dst != 63)
                    def _():
                        copy(i, lo, hi, start + lo)
                else:
                    copy(i, lo, hi, start + lo)
            return carry

        lax.fori_loop(0, 32, send, 0)

    send_part(0)

    wrow.wait()
    wcols = [
        pltpu.make_async_remote_copy(
            wgt.at[pl.ds(0, WIN), pl.ds(at, 1)],
            wgt.at[pl.ds(0, WIN), pl.ds(to, 1)],
            wcol_sem.at[0, i], wcol_sem.at[1, i], device_id=(dev, lat), device_id_type=MESH,
        )
        for i, (at, to, dev) in enumerate(((HALO + CHUNKS, HALO, east), (HALO + 1, HALO + 1 + CHUNKS, west)))
    ]
    for c in wcols:
        c.start()
    for part in range(1, PARTS):
        send_part(part)

    lane = lax.broadcasted_iota(jnp.int32, (8, LANES), 1)
    is_first, is_last = lane == 0, lane == LANES - 1

    def at(ref, w, q):
        return ref[w, pl.ds(q, 8), :]

    def to_east(ref, w, q, mid):
        nxt = at(ref, w, q + 1)
        return pltpu.roll(jnp.where(is_first, nxt, mid), LANES - 1, 1)

    def to_west(ref, w, q, mid):
        prv = at(ref, w, q - 1)
        return pltpu.roll(jnp.where(is_last, prv, mid), 1, 1)

    def dual_row(step, w, q, mid, below):
        weight = at(wgt, w, q)
        ux = to_east(surf if step == 0 else height, w, q, mid) - mid
        uy = jnp.zeros_like(mid) if below is None else below - mid
        if step == 0:
            qx, qy = STEP * ux, STEP * uy
        else:
            qx = at(dual_x, w, q) + STEP * (2.0 * ux - at(slope_x, w, q))
            qy = at(dual_y, w, q) + STEP * (2.0 * uy - at(slope_y, w, q))
        if step < ITERS - 1:
            slope_x[w, pl.ds(q, 8), :] = ux
            slope_y[w, pl.ds(q, 8), :] = uy
        shrink = jnp.minimum(1.0, weight * lax.rsqrt(qx * qx + qy * qy))
        px, py = qx * shrink, qy * shrink
        dual_x[w, pl.ds(q, 8), :] = px
        dual_y[w, pl.ds(q, 8), :] = py
        return px, py, weight * jnp.sqrt(ux * ux + uy * uy)

    def primal_row(step, w, q, height_ref, py_north):
        px, py = at(dual_x, w, q), at(dual_y, w, q)
        d = px - to_west(dual_x, w, q, px) + py
        if py_north is not None:
            d = d - py_north
        h, s, f = at(height_ref, w, q), at(surf, w, q), at(fid, w, q)
        scaled = STEP * f
        damp = 1.0 + scaled
        both = 1.0 / (f * damp)
        term = d * (s + (0.5 * d) * (both * damp))
        if step > 0:
            miss = h - s
            term = term + (0.5 * f) * (miss * miss)
        new = (h + STEP * d + scaled * s) * (both * f)
        return new, term

    def count(step, g, terms):
        def total(rows):
            found = [terms[w] for w in rows if w in terms]
            return functools.reduce(jnp.add, found) if found else None

        parts = [total(range(3, 32))]
        for rows, cond in ((range(3), lat == 0), (range(32, WIN), lat == 1)):
            some = total(rows)
            if some is not None:
                parts.append(jnp.where(cond, some, 0.0))
        some = functools.reduce(jnp.add, [p for p in parts if p is not None])
        in_tile = (g > FIRST) & (g < LAST)
        return jnp.where(in_tile, some, 0.0)

    def place(w, g):
        r = jnp.clip(w - first, 0, ROWS - 1)
        return pl.ds(r // 8 * 640 + r % 8 + (g - FIRST - 1) * 64, 8, stride=8)

    def duals(step, rows, g, write=True):
        ref = surf if step == 0 else height
        q = pl.multiple_of(8 * g, 8)
        terms, seen = {}, {}

        def row(w):
            if w not in seen:
                seen[w] = at(ref, w, q)
            return seen[w]

        for w in rows:
            below = row(w + 1) if w < WIN - 1 else None
            px, py, terms[w] = dual_row(step, w, q, row(w), below)
            if step == ITERS - 1 and write:
                out_x[place(w, g), :] = px
                out_y[place(w, g), :] = py
        return count(step, g, terms)

    def primals(step, rows, g, write=True):
        q = pl.multiple_of(8 * g, 8)
        terms = {}
        for w in rows:
            north = at(dual_y, w - 1, q) if w > 0 else None
            new, terms[w] = primal_row(step, w, q, surf if step == 0 else height, north)
            if step < ITERS - 1:
                height[w, pl.ds(q, 8), :] = new
            else:
                out_h[place(w, g), :] = new
        return count(step, g, terms)

    def stage(fn, step, rows, g0, g1, write=True):
        batch = max(1, 36 // len(rows))
        whole = max(g1 - g0, 0) // batch

        def body(g, n):
            terms = [fn(step, rows, g + i, write) for i in range(n)]
            acc[step] += functools.reduce(jnp.add, terms)

        def go(k, carry):
            body(g0 + k * batch, batch)
            return carry

        if whole:
            lax.fori_loop(0, whole, go, 0)
        if g0 + whole * batch < g1:
            body(jnp.int32(g0 + whole * batch), g1 - g0 - whole * batch)

    def sweep(inner, part):
        done = FIRST if part == 0 else stop_of(part - 1)
        stop = stop_of(part)
        final = part == PARTS - 1

        def rows(low, high):
            if inner:
                return list(range(low, high + 1))
            return list(range(0, low)) + list(range(WIN - 1, high, -1))

        for step in range(ITERS):
            g0 = max(done - step, FIRST)
            g1 = stop if final else stop - step
            if step == ITERS - 1:
                g1 = min(g1, LAST)
                if g0 == FIRST:
                    stage(duals, step, rows(3 + step, 30 - step), g0, g0 + 1, False)
                    g0 += 1
            stage(duals, step, rows(3 + step, 30 - step), g0, g1)
            stage(primals, step, rows(4 + step, 30 - step), g0, g1)

    def stop_of(part):
        return LAST + 1 if part == PARTS - 1 else (HALO + CUTS[part + 1] - 9) // 8 + 1

    for step in range(ITERS):
        acc[step] = jnp.zeros((8, LANES), jnp.float32)

    def relays(part):
        lo, n = HALO + CUTS[part], CUTS[part + 1] - CUTS[part]
        return [
            row_copy(ref, depth, lo, n, relay_send.at[i, part], relay_recv.at[i, part])
            for i, (ref, depth) in enumerate(((surf, 3), (fid, 2)))
        ]

    def finish(part):
        for c in relays(part):
            c.wait()
        sweep(False, part)

    for part in range(PARTS):
        lo, n = HALO + CUTS[part], CUTS[part + 1] - CUTS[part]
        for i, ref in enumerate((surf, fid)):
            got = ref.at[pl.ds(0, ROWS), pl.ds(lo, n)]
            pltpu.make_async_copy(got, got, recv_sem.at[i, part]).wait()
        for c in relays(part):
            c.start()
        if part == 0:
            for c in wcols:
                c.wait()
        sweep(True, part)
        if part > 0:
            finish(part - 1)
    finish(PARTS - 1)

    def total_of(ref, n):
        total = ref[0]
        for k in range(1, n):
            total = total + ref[k]
        return total

    rows = [jnp.sum(acc[step], axis=0, keepdims=True) for step in range(ITERS)]
    slots_a[0] = jnp.concatenate(rows + [jnp.zeros((5, LANES), jnp.float32)], axis=0)

    def spread(slots, n, peer, which):
        def go(k, carry):
            pltpu.make_async_remote_copy(
                slots.at[0], slots.at[k], gap_send.at[which], gap_recv.at[which],
                device_id=peer(k), device_id_type=MESH,
            ).start()
            return carry

        lax.fori_loop(1, n, go, 0)
        rest = slots.at[pl.ds(1, n - 1)]
        pltpu.make_async_copy(rest, rest, gap_recv.at[which]).wait()
        pltpu.make_async_copy(rest, rest, gap_send.at[which]).wait()

    spread(slots_a, 8, peer_a, 0)
    slots_b[0] = total_of(slots_a, 8)
    spread(slots_b, 16, peer_b, 1)
    gap_out[...] = jnp.sum(total_of(slots_b, 16), axis=1, keepdims=True) * (
        1.0 / (2 * ROWS * LINE * LANES)
    ) + jnp.zeros((8, LANES), jnp.float32)

    for i, ref in enumerate((surf, fid)):
        for n, cond in ((31, own), (32, jnp.logical_not(own))):
            @pl.when(cond)
            def _():
                sent = ref.at[pl.ds(0, n), pl.ds(0, CHUNKS + 2)]
                pltpu.make_async_copy(sent, sent, send_sem.at[i]).wait()


def on_device(surface, fidelity, smoothing):
    tile = smoothing.reshape(4, 8, CHUNKS, LANES).transpose(0, 2, 1, 3).reshape(-1, LANES)
    window = pltpu.VMEM((WIN, PITCH, LANES), jnp.float32)
    flat = jax.ShapeDtypeStruct((ROWS * CHUNKS, LANES), jnp.float32)
    *outs, gap = pl.pallas_call(
        kernel,
        out_shape=[flat] * 3 + [jax.ShapeDtypeStruct((8, LANES), jnp.float32)],
        in_specs=[pl.BlockSpec(memory_space=pltpu.HBM)] * 3,
        out_specs=[pl.BlockSpec(memory_space=pltpu.VMEM)] * 4,
        scratch_shapes=[window] * 3
        + [pltpu.VMEM((ROWS * CHUNKS, LANES), jnp.float32)]
        + [window] * 5
        + [
            pltpu.VMEM((ITERS, 8, LANES), jnp.float32),
            pltpu.VMEM((8, 8, LANES), jnp.float32),
            pltpu.VMEM((16, 8, LANES), jnp.float32),
            pltpu.SemaphoreType.DMA((2,)),
            pltpu.SemaphoreType.DMA((2, PARTS)),
            pltpu.SemaphoreType.DMA((2, PARTS)),
            pltpu.SemaphoreType.DMA((2, PARTS)),
            pltpu.SemaphoreType.DMA((2,)),
            pltpu.SemaphoreType.DMA((2, 2)),
            pltpu.SemaphoreType.DMA,
            pltpu.SemaphoreType.DMA((2,)),
            pltpu.SemaphoreType.DMA((2,)),
        ],
        compiler_params=pltpu.CompilerParams(
            collective_id=0, has_side_effects=True, vmem_limit_bytes=48 * 2**20
        ),
    )(surface.reshape(LINE, LANES), fidelity.reshape(LINE, LANES), tile)
    tiles = [
        o.reshape(4, CHUNKS, 8, LANES).transpose(0, 2, 1, 3).reshape(ROWS, CHUNKS * LANES)
        for o in outs
    ]
    return (*tiles, gap[:ITERS, 0])


def solution(mesh):
    in_specs = (P("lon", None), P("lon", None), P("lat", "lon"))
    out_specs = (P("lat", "lon"), P("lat", "lon"), P("lat", "lon"), P())
    return jax.shard_map(
        on_device, mesh=mesh, in_specs=in_specs, out_specs=out_specs, check_vma=False
    )
```

```python
import functools

import jax
import jax.numpy as jnp
from jax import lax
from jax.experimental import pallas as pl
from jax.experimental.pallas import tpu as pltpu
from jax.sharding import PartitionSpec as P

MESH = pl.DeviceIdType.MESH
STEP = 0.35
ITERS = 3
LANES = 128
ROWS = 32
CHUNKS = 80
LINE = 5120
WIN = 35
HALO = 15
PITCH = 112
CUTS = (0, 26, 50, 74, 82)
PARTS = len(CUTS) - 1
FIRST, LAST = 1, 12


def kernel(
    surf_hbm, fid_hbm, smooth_hbm,
    out_h, out_x, out_y, gap_out,
    surf, fid, wgt, tile_in, height, dual_x, dual_y, slope_x, slope_y,
    acc, slots_a, slots_b,
    send_sem, recv_sem, relay_send, relay_recv, halo_sem, tile_sem, gap_send, gap_recv,
):
    lon = lax.axis_index("lon")
    lat = lax.axis_index("lat")
    core, x, zlo, y = lon % 2, (lon // 2) % 4, (lon // 8) % 2, lon // 16
    half = y // 2
    z_to = (zlo + lat + half) % 2
    own = lat == half
    slot = lon - 29 * half
    first = 3 * lat

    def lon_of(y_, zlo_, x_, core_):
        return ((y_ * 2 + zlo_) * 4 + x_) * 2 + core_

    tile_copy = pltpu.make_async_copy(smooth_hbm, tile_in, tile_sem)
    tile_copy.start()

    barrier = pltpu.get_barrier_semaphore()

    def greet(lon_, lat_):
        pl.semaphore_signal(barrier, inc=1, device_id=(lon_, lat_), device_id_type=MESH)

    def greet_source(k, carry):
        zs = (zlo + k) % 2
        zh = jnp.where(zs == zlo, lat, 1 - lat)
        src = lon_of(2 * lat + (k // 2) % 2, zs, (x + k // 8) % 4, (core + k // 4) % 2)

        @pl.when((src != lon) | (zh != lat))
        def _():
            greet(src, zh)

        return carry

    lax.fori_loop(0, 32, greet_source, 0)
    east, west = (lon + 1) % 64, (lon + 63) % 64
    greet(lon, 1 - lat)
    for lat_ in (lat, 1 - lat):
        greet(east, lat_)
        greet(west, lat_)

    def peer_a(k):
        return lon_of(y, zlo, (x + k // 2) % 4, (core + k) % 2), lat

    def peer_b(k):
        return lon_of((y + k // 4) % 4, (zlo + k // 2) % 2, x, core), (lat + k) % 2

    def greet_a(k, carry):
        greet(*peer_a(k))
        return carry

    def greet_b(k, carry):
        greet(*peer_b(k))
        return carry

    lax.fori_loop(1, 8, greet_a, 0)
    lax.fori_loop(1, 16, greet_b, 0)

    tile_copy.wait()

    def lay(k, carry):
        blk, g = k // 10, k % 10
        for r8 in range(8):
            wgt[first + blk * 8 + r8, pl.ds(16 + 8 * g, 8), :] = tile_in[
                pl.ds(blk * 640 + g * 64 + r8, 8, stride=8), :
            ]
        return carry

    lax.fori_loop(0, 40, lay, 0)

    n_self = own.astype(jnp.int32)
    pl.semaphore_wait(barrier, 32 - n_self + 5 + 7 + 15)

    def row_copy(ref, depth, lo, n, s_sem, r_sem):
        give = (32 - depth) * (1 - lat) + 3 * lat
        put = (3 - depth) * (1 - lat) + 32 * lat
        return pltpu.make_async_remote_copy(
            ref.at[pl.ds(give, depth), pl.ds(lo, n)],
            ref.at[pl.ds(put, depth), pl.ds(lo, n)],
            s_sem, r_sem, device_id=(lon, 1 - lat), device_id_type=MESH,
        )

    give_w, put_w = 29 * (1 - lat) + 3 * lat, 32 * lat
    halo = [
        pltpu.make_async_remote_copy(
            wgt.at[pl.ds(give_w, 3), pl.ds(HALO + 1, CHUNKS)],
            wgt.at[pl.ds(put_w, 3), pl.ds(HALO + 1, CHUNKS)],
            halo_sem.at[0, 0], halo_sem.at[1, 0], device_id=(lon, 1 - lat), device_id_type=MESH,
        )
    ]
    for i, (q0, q1, dev) in enumerate(
        ((HALO + CHUNKS, HALO, east), (HALO + 1, HALO + 1 + CHUNKS, west))
    ):
        for j, (w0, w1, n, lat_) in enumerate(
            ((first, first, ROWS, lat), (give_w, put_w, 3, 1 - lat))
        ):
            k = 1 + 2 * i + j
            halo.append(
                pltpu.make_async_remote_copy(
                    wgt.at[pl.ds(w0, n), pl.ds(q0, 1)],
                    wgt.at[pl.ds(w1, n), pl.ds(q1, 1)],
                    halo_sem.at[0, k], halo_sem.at[1, k],
                    device_id=(dev, lat_), device_id_type=MESH,
                )
            )
    for c in halo:
        c.start()

    def send_part(part):
        lo, hi = CUTS[part], CUTS[part + 1]

        def send(k, carry):
            dx = (k + 1) % 4
            dy = ((k % 16) // 4 + 4 - dx) % 4
            dst = lon_of((y + dy) % 4, z_to, (x + dx) % 4, (core + k // 16) % 2)
            here = (k == 3) & own

            def copy(i, a, b, at):
                src_ref = (surf_hbm, fid_hbm)[i].at[pl.ds(at, b - a)]
                dst_ref = (surf, fid)[i].at[slot, pl.ds(HALO + a, b - a)]

                @pl.when(here)
                def _():
                    pltpu.make_async_copy(src_ref, dst_ref, recv_sem.at[i, part]).start()

                @pl.when(jnp.logical_not(here))
                def _():
                    pltpu.make_async_remote_copy(
                        src_ref, dst_ref, send_sem.at[i], recv_sem.at[i, part],
                        device_id=(dst, half), device_id_type=MESH,
                    ).start()

            for i in range(2):
                start = dst * CHUNKS - 1
                if lo == 0:
                    @pl.when(dst == 0)
                    def _():
                        copy(i, 0, 1, LINE - 1)
                        copy(i, 1, hi, 0)

                    @pl.when(dst != 0)
                    def _():
                        copy(i, 0, hi, start)
                elif hi == CHUNKS + 2:
                    @pl.when(dst == 63)
                    def _():
                        copy(i, lo, hi - 1, LINE - CHUNKS - 1 + lo)
                        copy(i, hi - 1, hi, 0)

                    @pl.when(dst != 63)
                    def _():
                        copy(i, lo, hi, start + lo)
                else:
                    copy(i, lo, hi, start + lo)
            return carry

        lax.fori_loop(0, 32, send, 0)

    for part in range(PARTS):
        send_part(part)

    lane = lax.broadcasted_iota(jnp.int32, (8, LANES), 1)
    is_first, is_last = lane == 0, lane == LANES - 1

    def at(ref, w, q):
        return ref[w, pl.ds(q, 8), :]

    def to_east(ref, w, q, mid):
        nxt = at(ref, w, q + 1)
        return pltpu.roll(jnp.where(is_first, nxt, mid), LANES - 1, 1)

    def to_west(ref, w, q, mid):
        prv = at(ref, w, q - 1)
        return pltpu.roll(jnp.where(is_last, prv, mid), 1, 1)

    def dual_row(step, w, q, mid, below):
        weight = at(wgt, w, q)
        ux = to_east(surf if step == 0 else height, w, q, mid) - mid
        uy = jnp.zeros_like(mid) if below is None else below - mid
        if step == 0:
            qx, qy = STEP * ux, STEP * uy
        else:
            qx = at(dual_x, w, q) + STEP * (2.0 * ux - at(slope_x, w, q))
            qy = at(dual_y, w, q) + STEP * (2.0 * uy - at(slope_y, w, q))
        if step < ITERS - 1:
            slope_x[w, pl.ds(q, 8), :] = ux
            slope_y[w, pl.ds(q, 8), :] = uy
        shrink = jnp.minimum(1.0, weight * lax.rsqrt(qx * qx + qy * qy))
        px, py = qx * shrink, qy * shrink
        dual_x[w, pl.ds(q, 8), :] = px
        dual_y[w, pl.ds(q, 8), :] = py
        return px, py, weight * jnp.sqrt(ux * ux + uy * uy)

    def primal_row(step, w, q, height_ref, py_north):
        px, py = at(dual_x, w, q), at(dual_y, w, q)
        d = px - to_west(dual_x, w, q, px) + py
        if py_north is not None:
            d = d - py_north
        h, s, f = at(height_ref, w, q), at(surf, w, q), at(fid, w, q)
        scaled = STEP * f
        damp = 1.0 + scaled
        both = 1.0 / (f * damp)
        term = d * (s + (0.5 * d) * (both * damp))
        if step > 0:
            miss = h - s
            term = term + (0.5 * f) * (miss * miss)
        new = (h + STEP * d + scaled * s) * (both * f)
        return new, term

    def count(step, g, terms):
        def total(rows):
            found = [terms[w] for w in rows if w in terms]
            return functools.reduce(jnp.add, found) if found else None

        parts = [total(range(3, 32))]
        for rows, cond in ((range(3), lat == 0), (range(32, WIN), lat == 1)):
            some = total(rows)
            if some is not None:
                parts.append(jnp.where(cond, some, 0.0))
        some = functools.reduce(jnp.add, [p for p in parts if p is not None])
        in_tile = (g > FIRST) & (g < LAST)
        return jnp.where(in_tile, some, 0.0)

    def place(w, g):
        r = jnp.clip(w - first, 0, ROWS - 1)
        return pl.ds(r // 8 * 640 + r % 8 + (g - FIRST - 1) * 64, 8, stride=8)

    def duals(step, rows, g, write=True):
        ref = surf if step == 0 else height
        q = pl.multiple_of(8 * g, 8)
        terms, seen = {}, {}

        def row(w):
            if w not in seen:
                seen[w] = at(ref, w, q)
            return seen[w]

        for w in rows:
            below = row(w + 1) if w < WIN - 1 else None
            px, py, terms[w] = dual_row(step, w, q, row(w), below)
            if step == ITERS - 1 and write:
                out_x[place(w, g), :] = px
                out_y[place(w, g), :] = py
        return count(step, g, terms)

    def primals(step, rows, g, write=True):
        q = pl.multiple_of(8 * g, 8)
        terms = {}
        for w in rows:
            north = at(dual_y, w - 1, q) if w > 0 else None
            new, terms[w] = primal_row(step, w, q, surf if step == 0 else height, north)
            if step < ITERS - 1:
                height[w, pl.ds(q, 8), :] = new
            else:
                out_h[place(w, g), :] = new
        return count(step, g, terms)

    def stage(fn, step, rows, g0, g1, write=True):
        batch = max(1, 36 // len(rows))
        whole = max(g1 - g0, 0) // batch

        def body(g, n):
            terms = [fn(step, rows, g + i, write) for i in range(n)]
            acc[step] += functools.reduce(jnp.add, terms)

        def go(k, carry):
            body(g0 + k * batch, batch)
            return carry

        if whole:
            lax.fori_loop(0, whole, go, 0)
        if g0 + whole * batch < g1:
            body(jnp.int32(g0 + whole * batch), g1 - g0 - whole * batch)

    def sweep(inner, part):
        done = FIRST if part == 0 else stop_of(part - 1)
        stop = stop_of(part)
        final = part == PARTS - 1

        def rows(low, high):
            if inner:
                return list(range(low, high + 1))
            return list(range(0, low)) + list(range(WIN - 1, high, -1))

        for step in range(ITERS):
            g0 = max(done - step, FIRST)
            g1 = stop if final else stop - step
            if step == ITERS - 1:
                g1 = min(g1, LAST)
                if g0 == FIRST:
                    stage(duals, step, rows(3 + step, 30 - step), g0, g0 + 1, False)
                    g0 += 1
            stage(duals, step, rows(3 + step, 30 - step), g0, g1)
            stage(primals, step, rows(4 + step, 30 - step), g0, g1)

    def stop_of(part):
        return LAST + 1 if part == PARTS - 1 else (HALO + CUTS[part + 1] - 9) // 8 + 1

    for step in range(ITERS):
        acc[step] = jnp.zeros((8, LANES), jnp.float32)

    def relays(part):
        lo, n = HALO + CUTS[part], CUTS[part + 1] - CUTS[part]
        return [
            row_copy(ref, depth, lo, n, relay_send.at[i, part], relay_recv.at[i, part])
            for i, (ref, depth) in enumerate(((surf, 3), (fid, 2)))
        ]

    def finish(part):
        for c in relays(part):
            c.wait()
        sweep(False, part)

    for part in range(PARTS):
        lo, n = HALO + CUTS[part], CUTS[part + 1] - CUTS[part]
        for i, ref in enumerate((surf, fid)):
            got = ref.at[pl.ds(0, ROWS), pl.ds(lo, n)]
            pltpu.make_async_copy(got, got, recv_sem.at[i, part]).wait()
        for c in relays(part):
            c.start()
        if part == 0:
            for c in halo:
                c.wait()
        sweep(True, part)
        if part > 0:
            finish(part - 1)
    finish(PARTS - 1)

    def total_of(ref, n):
        total = ref[0]
        for k in range(1, n):
            total = total + ref[k]
        return total

    rows = [jnp.sum(acc[step], axis=0, keepdims=True) for step in range(ITERS)]
    slots_a[0] = jnp.concatenate(rows + [jnp.zeros((5, LANES), jnp.float32)], axis=0)

    def spread(slots, n, peer, which):
        def go(k, carry):
            pltpu.make_async_remote_copy(
                slots.at[0], slots.at[k], gap_send.at[which], gap_recv.at[which],
                device_id=peer(k), device_id_type=MESH,
            ).start()
            return carry

        lax.fori_loop(1, n, go, 0)
        rest = slots.at[pl.ds(1, n - 1)]
        pltpu.make_async_copy(rest, rest, gap_recv.at[which]).wait()
        pltpu.make_async_copy(rest, rest, gap_send.at[which]).wait()

    spread(slots_a, 8, peer_a, 0)
    slots_b[0] = total_of(slots_a, 8)
    spread(slots_b, 16, peer_b, 1)
    gap_out[...] = jnp.sum(total_of(slots_b, 16), axis=1, keepdims=True) * (
        1.0 / (2 * ROWS * LINE * LANES)
    ) + jnp.zeros((8, LANES), jnp.float32)

    for i, ref in enumerate((surf, fid)):
        for n, cond in ((31, own), (32, jnp.logical_not(own))):
            @pl.when(cond)
            def _():
                sent = ref.at[pl.ds(0, n), pl.ds(0, CHUNKS + 2)]
                pltpu.make_async_copy(sent, sent, send_sem.at[i]).wait()


def on_device(surface, fidelity, smoothing):
    tile = smoothing.reshape(4, 8, CHUNKS, LANES).transpose(0, 2, 1, 3).reshape(-1, LANES)
    window = pltpu.VMEM((WIN, PITCH, LANES), jnp.float32)
    flat = jax.ShapeDtypeStruct((ROWS * CHUNKS, LANES), jnp.float32)
    *outs, gap = pl.pallas_call(
        kernel,
        out_shape=[flat] * 3 + [jax.ShapeDtypeStruct((8, LANES), jnp.float32)],
        in_specs=[pl.BlockSpec(memory_space=pltpu.HBM)] * 3,
        out_specs=[pl.BlockSpec(memory_space=pltpu.VMEM)] * 4,
        scratch_shapes=[window] * 3
        + [pltpu.VMEM((ROWS * CHUNKS, LANES), jnp.float32)]
        + [window] * 5
        + [
            pltpu.VMEM((ITERS, 8, LANES), jnp.float32),
            pltpu.VMEM((8, 8, LANES), jnp.float32),
            pltpu.VMEM((16, 8, LANES), jnp.float32),
            pltpu.SemaphoreType.DMA((2,)),
            pltpu.SemaphoreType.DMA((2, PARTS)),
            pltpu.SemaphoreType.DMA((2, PARTS)),
            pltpu.SemaphoreType.DMA((2, PARTS)),
            pltpu.SemaphoreType.DMA((2, 5)),
            pltpu.SemaphoreType.DMA,
            pltpu.SemaphoreType.DMA((2,)),
            pltpu.SemaphoreType.DMA((2,)),
        ],
        compiler_params=pltpu.CompilerParams(
            collective_id=0, has_side_effects=True, vmem_limit_bytes=48 * 2**20
        ),
    )(surface.reshape(LINE, LANES), fidelity.reshape(LINE, LANES), tile)
    tiles = [
        o.reshape(4, CHUNKS, 8, LANES).transpose(0, 2, 1, 3).reshape(ROWS, CHUNKS * LANES)
        for o in outs
    ]
    return (*tiles, gap[:ITERS, 0])


def solution(mesh):
    in_specs = (P("lon", None), P("lon", None), P("lat", "lon"))
    out_specs = (P("lat", "lon"), P("lat", "lon"), P("lat", "lon"), P())
    return jax.shard_map(
        on_device, mesh=mesh, in_specs=in_specs, out_specs=out_specs, check_vma=False
    )
```

```python
import functools

import jax
import jax.numpy as jnp
from jax import lax
from jax.experimental import pallas as pl
from jax.experimental.pallas import tpu as pltpu
from jax.sharding import PartitionSpec as P

MESH = pl.DeviceIdType.MESH
STEP = 0.35
ITERS = 3
LANES = 128
ROWS = 32
CHUNKS = 80
LINE = 5120
WIN = 35
HALO = 15
PITCH = 112
CUTS = (0, 26, 50, 74, 82)
PARTS = len(CUTS) - 1
FIRST, LAST = 1, 12


def kernel(
    surf_hbm, fid_hbm, smooth_hbm,
    out_h, out_x, out_y, gap_out,
    surf, fid, wgt, tile_in, height, dual_x, dual_y, slope_x, slope_y,
    acc, slots_a, slots_b,
    send_sem, recv_sem, relay_send, relay_recv, halo_sem, tile_sem, gap_send, gap_recv,
):
    lon = lax.axis_index("lon")
    lat = lax.axis_index("lat")
    core, x, zlo, y = lon % 2, (lon // 2) % 4, (lon // 8) % 2, lon // 16
    half = y // 2
    z_to = (zlo + lat + half) % 2
    own = lat == half
    slot = lon - 29 * half
    first = 3 * lat

    def lon_of(y_, zlo_, x_, core_):
        return ((y_ * 2 + zlo_) * 4 + x_) * 2 + core_

    tile_copy = pltpu.make_async_copy(smooth_hbm, tile_in, tile_sem)
    tile_copy.start()

    barrier = pltpu.get_barrier_semaphore()

    def greet(lon_, lat_):
        pl.semaphore_signal(barrier, inc=1, device_id=(lon_, lat_), device_id_type=MESH)

    def greet_source(k, carry):
        zs = (zlo + k) % 2
        zh = jnp.where((zs == zlo) | (k < 8), lat, 1 - lat)
        src = lon_of(2 * lat + (k // 2) % 2, zs, (x + k // 8) % 4, (core + k // 4) % 2)

        @pl.when((src != lon) | (zh != lat))
        def _():
            greet(src, zh)

        return carry

    lax.fori_loop(0, 32, greet_source, 0)
    east, west = (lon + 1) % 64, (lon + 63) % 64
    greet(lon, 1 - lat)
    for lat_ in (lat, 1 - lat):
        greet(east, lat_)
        greet(west, lat_)

    def peer_a(k):
        return lon_of(y, zlo, (x + k // 2) % 4, (core + k) % 2), lat

    def peer_b(k):
        return lon_of((y + k // 4) % 4, (zlo + k // 2) % 2, x, core), (lat + k) % 2

    def greet_a(k, carry):
        greet(*peer_a(k))
        return carry

    def greet_b(k, carry):
        greet(*peer_b(k))
        return carry

    lax.fori_loop(1, 8, greet_a, 0)
    lax.fori_loop(1, 16, greet_b, 0)

    tile_copy.wait()

    def lay(k, carry):
        blk, g = k // 10, k % 10
        for r8 in range(8):
            wgt[first + blk * 8 + r8, pl.ds(16 + 8 * g, 8), :] = tile_in[
                pl.ds(blk * 640 + g * 64 + r8, 8, stride=8), :
            ]
        return carry

    lax.fori_loop(0, 40, lay, 0)

    pl.semaphore_wait(barrier, jnp.where(own, 39, 24) + 5 + 7 + 15)

    def row_copy(ref, depth, lo, n, s_sem, r_sem):
        give = (32 - depth) * (1 - lat) + 3 * lat
        put = (3 - depth) * (1 - lat) + 32 * lat
        return pltpu.make_async_remote_copy(
            ref.at[pl.ds(give, depth), pl.ds(lo, n)],
            ref.at[pl.ds(put, depth), pl.ds(lo, n)],
            s_sem, r_sem, device_id=(lon, 1 - lat), device_id_type=MESH,
        )

    give_w, put_w = 29 * (1 - lat) + 3 * lat, 32 * lat
    halo = [
        pltpu.make_async_remote_copy(
            wgt.at[pl.ds(give_w, 3), pl.ds(HALO + 1, CHUNKS)],
            wgt.at[pl.ds(put_w, 3), pl.ds(HALO + 1, CHUNKS)],
            halo_sem.at[0, 0], halo_sem.at[1, 0], device_id=(lon, 1 - lat), device_id_type=MESH,
        )
    ]
    for i, (q0, q1, dev) in enumerate(
        ((HALO + CHUNKS, HALO, east), (HALO + 1, HALO + 1 + CHUNKS, west))
    ):
        for j, (w0, w1, n, lat_) in enumerate(
            ((first, first, ROWS, lat), (give_w, put_w, 3, 1 - lat))
        ):
            k = 1 + 2 * i + j
            halo.append(
                pltpu.make_async_remote_copy(
                    wgt.at[pl.ds(w0, n), pl.ds(q0, 1)],
                    wgt.at[pl.ds(w1, n), pl.ds(q1, 1)],
                    halo_sem.at[0, k], halo_sem.at[1, k],
                    device_id=(dev, lat_), device_id_type=MESH,
                )
            )
    for c in halo:
        c.start()

    def send_part(part):
        lo, hi = CUTS[part], CUTS[part + 1]

        def send(step, carry):
            k, extra = step // 2, step % 2 == 1
            dx = (k + 1) % 4
            dy = ((k % 16) // 4 + 4 - dx) % 4
            z_dst = jnp.where(extra, 1 - zlo, z_to)
            dst = lon_of((y + dy) % 4, z_dst, (x + dx) % 4, (core + k // 16) % 2)
            here = (step == 6) & own

            @pl.when(jnp.where(extra, own & (dx == 0), own | (dx != 0)))
            def _():
                send_block(dst, here)

            return carry

        def send_block(dst, here):
            def copy(i, a, b, at):
                src_ref = (surf_hbm, fid_hbm)[i].at[pl.ds(at, b - a)]
                dst_ref = (surf, fid)[i].at[slot, pl.ds(HALO + a, b - a)]

                @pl.when(here)
                def _():
                    pltpu.make_async_copy(src_ref, dst_ref, recv_sem.at[i, part]).start()

                @pl.when(jnp.logical_not(here))
                def _():
                    pltpu.make_async_remote_copy(
                        src_ref, dst_ref, send_sem.at[i], recv_sem.at[i, part],
                        device_id=(dst, half), device_id_type=MESH,
                    ).start()

            for i in range(2):
                start = dst * CHUNKS - 1
                if lo == 0:
                    @pl.when(dst == 0)
                    def _():
                        copy(i, 0, 1, LINE - 1)
                        copy(i, 1, hi, 0)

                    @pl.when(dst != 0)
                    def _():
                        copy(i, 0, hi, start)
                elif hi == CHUNKS + 2:
                    @pl.when(dst == 63)
                    def _():
                        copy(i, lo, hi - 1, LINE - CHUNKS - 1 + lo)
                        copy(i, hi - 1, hi, 0)

                    @pl.when(dst != 63)
                    def _():
                        copy(i, lo, hi, start + lo)
                else:
                    copy(i, lo, hi, start + lo)

        lax.fori_loop(0, 64, send, 0)

    for part in range(PARTS):
        send_part(part)

    lane = lax.broadcasted_iota(jnp.int32, (8, LANES), 1)
    is_first, is_last = lane == 0, lane == LANES - 1

    def at(ref, w, q):
        return ref[w, pl.ds(q, 8), :]

    def to_east(ref, w, q, mid):
        nxt = at(ref, w, q + 1)
        return pltpu.roll(jnp.where(is_first, nxt, mid), LANES - 1, 1)

    def to_west(ref, w, q, mid):
        prv = at(ref, w, q - 1)
        return pltpu.roll(jnp.where(is_last, prv, mid), 1, 1)

    def dual_row(step, w, q, mid, below):
        weight = at(wgt, w, q)
        ux = to_east(surf if step == 0 else height, w, q, mid) - mid
        uy = jnp.zeros_like(mid) if below is None else below - mid
        if step == 0:
            qx, qy = STEP * ux, STEP * uy
        else:
            qx = at(dual_x, w, q) + STEP * (2.0 * ux - at(slope_x, w, q))
            qy = at(dual_y, w, q) + STEP * (2.0 * uy - at(slope_y, w, q))
        if step < ITERS - 1:
            slope_x[w, pl.ds(q, 8), :] = ux
            slope_y[w, pl.ds(q, 8), :] = uy
        shrink = jnp.minimum(1.0, weight * lax.rsqrt(qx * qx + qy * qy))
        px, py = qx * shrink, qy * shrink
        dual_x[w, pl.ds(q, 8), :] = px
        dual_y[w, pl.ds(q, 8), :] = py
        return px, py, weight * jnp.sqrt(ux * ux + uy * uy)

    def primal_row(step, w, q, height_ref, py_north):
        px, py = at(dual_x, w, q), at(dual_y, w, q)
        d = px - to_west(dual_x, w, q, px) + py
        if py_north is not None:
            d = d - py_north
        h, s, f = at(height_ref, w, q), at(surf, w, q), at(fid, w, q)
        scaled = STEP * f
        damp = 1.0 + scaled
        both = 1.0 / (f * damp)
        term = d * (s + (0.5 * d) * (both * damp))
        if step > 0:
            miss = h - s
            term = term + (0.5 * f) * (miss * miss)
        new = (h + STEP * d + scaled * s) * (both * f)
        return new, term

    def count(step, g, terms):
        def total(rows):
            found = [terms[w] for w in rows if w in terms]
            return functools.reduce(jnp.add, found) if found else None

        parts = [total(range(3, 32))]
        for rows, cond in ((range(3), lat == 0), (range(32, WIN), lat == 1)):
            some = total(rows)
            if some is not None:
                parts.append(jnp.where(cond, some, 0.0))
        some = functools.reduce(jnp.add, [p for p in parts if p is not None])
        in_tile = (g > FIRST) & (g < LAST)
        return jnp.where(in_tile, some, 0.0)

    def place(w, g):
        r = jnp.clip(w - first, 0, ROWS - 1)
        return pl.ds(r // 8 * 640 + r % 8 + (g - FIRST - 1) * 64, 8, stride=8)

    def duals(step, rows, g, write=True):
        ref = surf if step == 0 else height
        q = pl.multiple_of(8 * g, 8)
        terms, seen = {}, {}

        def row(w):
            if w not in seen:
                seen[w] = at(ref, w, q)
            return seen[w]

        for w in rows:
            below = row(w + 1) if w < WIN - 1 else None
            px, py, terms[w] = dual_row(step, w, q, row(w), below)
            if step == ITERS - 1 and write:
                out_x[place(w, g), :] = px
                out_y[place(w, g), :] = py
        return count(step, g, terms)

    def primals(step, rows, g, write=True):
        q = pl.multiple_of(8 * g, 8)
        terms = {}
        for w in rows:
            north = at(dual_y, w - 1, q) if w > 0 else None
            new, terms[w] = primal_row(step, w, q, surf if step == 0 else height, north)
            if step < ITERS - 1:
                height[w, pl.ds(q, 8), :] = new
            else:
                out_h[place(w, g), :] = new
        return count(step, g, terms)

    def stage(fn, step, rows, g0, g1, write=True):
        batch = max(1, 36 // len(rows))
        whole = max(g1 - g0, 0) // batch

        def body(g, n):
            terms = [fn(step, rows, g + i, write) for i in range(n)]
            acc[step] += functools.reduce(jnp.add, terms)

        def go(k, carry):
            body(g0 + k * batch, batch)
            return carry

        if whole:
            lax.fori_loop(0, whole, go, 0)
        if g0 + whole * batch < g1:
            body(jnp.int32(g0 + whole * batch), g1 - g0 - whole * batch)

    def sweep(inner, part):
        done = FIRST if part == 0 else stop_of(part - 1)
        stop = stop_of(part)
        final = part == PARTS - 1

        def rows(low, high):
            if inner:
                return list(range(low, high + 1))
            return list(range(0, low)) + list(range(WIN - 1, high, -1))

        for step in range(ITERS):
            g0 = max(done - step, FIRST)
            g1 = stop if final else stop - step
            if step == ITERS - 1:
                g1 = min(g1, LAST)
                if g0 == FIRST:
                    stage(duals, step, rows(3 + step, 30 - step), g0, g0 + 1, False)
                    g0 += 1
            stage(duals, step, rows(3 + step, 30 - step), g0, g1)
            stage(primals, step, rows(4 + step, 30 - step), g0, g1)

    def stop_of(part):
        return LAST + 1 if part == PARTS - 1 else (HALO + CUTS[part + 1] - 9) // 8 + 1

    for step in range(ITERS):
        acc[step] = jnp.zeros((8, LANES), jnp.float32)

    def relay(part, i):
        lo, n = HALO + CUTS[part], CUTS[part + 1] - CUTS[part]
        ref, depth = ((surf, 3), (fid, 2))[i]
        return row_copy(ref, depth, lo, n, relay_send.at[i, part], relay_recv.at[i, part])

    def finish(part):
        for i in range(2):
            relay(part, i).wait()
        sweep(False, part)

    for part in range(PARTS):
        lo, n = HALO + CUTS[part], CUTS[part + 1] - CUTS[part]
        for i, ref in enumerate((surf, fid)):
            got = ref.at[pl.ds(0, ROWS), pl.ds(lo, n)]
            pltpu.make_async_copy(got, got, recv_sem.at[i, part]).wait()
            relay(part, i).start()
        if part == 0:
            for c in halo:
                c.wait()
        sweep(True, part)
        if part > 0:
            finish(part - 1)
    finish(PARTS - 1)

    def total_of(ref, n):
        total = ref[0]
        for k in range(1, n):
            total = total + ref[k]
        return total

    rows = [jnp.sum(acc[step], axis=0, keepdims=True) for step in range(ITERS)]
    slots_a[0] = jnp.concatenate(rows + [jnp.zeros((5, LANES), jnp.float32)], axis=0)

    def spread(slots, n, peer, which):
        def go(k, carry):
            pltpu.make_async_remote_copy(
                slots.at[0], slots.at[k], gap_send.at[which], gap_recv.at[which],
                device_id=peer(k), device_id_type=MESH,
            ).start()
            return carry

        lax.fori_loop(1, n, go, 0)
        rest = slots.at[pl.ds(1, n - 1)]
        pltpu.make_async_copy(rest, rest, gap_recv.at[which]).wait()
        pltpu.make_async_copy(rest, rest, gap_send.at[which]).wait()

    spread(slots_a, 8, peer_a, 0)
    slots_b[0] = total_of(slots_a, 8)
    spread(slots_b, 16, peer_b, 1)
    gap_out[...] = jnp.sum(total_of(slots_b, 16), axis=1, keepdims=True) * (
        1.0 / (2 * ROWS * LINE * LANES)
    ) + jnp.zeros((8, LANES), jnp.float32)

    for i, ref in enumerate((surf_hbm, fid_hbm)):
        for n, cond in ((39, own), (24, jnp.logical_not(own))):
            @pl.when(cond)
            def _():
                sent = ref.at[pl.ds(0, n * (CHUNKS + 2))]
                pltpu.make_async_copy(sent, sent, send_sem.at[i]).wait()


def on_device(surface, fidelity, smoothing):
    tile = smoothing.reshape(4, 8, CHUNKS, LANES).transpose(0, 2, 1, 3).reshape(-1, LANES)
    window = pltpu.VMEM((WIN, PITCH, LANES), jnp.float32)
    flat = jax.ShapeDtypeStruct((ROWS * CHUNKS, LANES), jnp.float32)
    *outs, gap = pl.pallas_call(
        kernel,
        out_shape=[flat] * 3 + [jax.ShapeDtypeStruct((8, LANES), jnp.float32)],
        in_specs=[pl.BlockSpec(memory_space=pltpu.HBM)] * 3,
        out_specs=[pl.BlockSpec(memory_space=pltpu.VMEM)] * 4,
        scratch_shapes=[window] * 3
        + [pltpu.VMEM((ROWS * CHUNKS, LANES), jnp.float32)]
        + [window] * 5
        + [
            pltpu.VMEM((ITERS, 8, LANES), jnp.float32),
            pltpu.VMEM((8, 8, LANES), jnp.float32),
            pltpu.VMEM((16, 8, LANES), jnp.float32),
            pltpu.SemaphoreType.DMA((2,)),
            pltpu.SemaphoreType.DMA((2, PARTS)),
            pltpu.SemaphoreType.DMA((2, PARTS)),
            pltpu.SemaphoreType.DMA((2, PARTS)),
            pltpu.SemaphoreType.DMA((2, 5)),
            pltpu.SemaphoreType.DMA,
            pltpu.SemaphoreType.DMA((2,)),
            pltpu.SemaphoreType.DMA((2,)),
        ],
        compiler_params=pltpu.CompilerParams(
            collective_id=0, has_side_effects=True, vmem_limit_bytes=48 * 2**20
        ),
    )(surface.reshape(LINE, LANES), fidelity.reshape(LINE, LANES), tile)
    tiles = [
        o.reshape(4, CHUNKS, 8, LANES).transpose(0, 2, 1, 3).reshape(ROWS, CHUNKS * LANES)
        for o in outs
    ]
    return (*tiles, gap[:ITERS, 0])


def solution(mesh):
    in_specs = (P("lon", None), P("lon", None), P("lat", "lon"))
    out_specs = (P("lat", "lon"), P("lat", "lon"), P("lat", "lon"), P())
    return jax.shard_map(
        on_device, mesh=mesh, in_specs=in_specs, out_specs=out_specs, check_vma=False
    )
```
